256 devices in a mesh: src: 16 (over y, x_lo, core), dst: 16 (over z, x_hi).
Axes of the slice: x: 4 (x_hi: 2, x_lo: 2; x = x_hi * 2 + x_lo), y: 4, z: 8, core: 2. Of those that a mesh axis runs over, the one named last changes fastest.
Arguments:
- raw: bfloat16 [32768, 256], P(('src', 'dst')), may hold values from -6 to 6
- enc_w1: bfloat16 [256, 512], replicated, may hold values from -0.375 to 0.375
- enc_w2: bfloat16 [512, 256], replicated, may hold values from -0.25 to 0.25
- block_weights: float32 [32768, 128, 128], P(('src', 'dst')), may hold values from -0.046875 to 0.046875
- block_cols: int32 [32768], P(('src', 'dst')), may hold values from 0 to 15, as said below
- noise: bfloat16 [3, 32768, 256], P(None, ('src', 'dst')), may hold values from -3 to 3
Outputs:
- encoded: bfloat16 [32768, 256], P(('src', 'dst'))
- hops: bfloat16 [3, 32768, 256], P(None, ('src', 'dst'))
The draws below stay inside these ranges and needn't reach their ends.
Inputs may be any that keep to these rules, and one draw needn't show every extreme that they name: `block_cols`: entry b of each device's 128 entries belongs to row block b // 8; row blocks 2j and 2j+1 of a device together name every column block exactly once, each naming 16 // 2 distinct ones.
All inputs are finite; a program needn't handle non-finite values.
Results may differ from the reference program's by a relative error of at most 0.0058.
Values may be sent and summed in bfloat16 or wider, within the bound.
No kernel may reach another device: no remote copies, remote signals or barrier semaphores. Data moves between devices by JAX's collectives and lax.ppermute only.
A program may use at most 128 MiB of HBM per device.

```python
import jax
import jax.numpy as jnp
from jax import lax

F_IN = 256
HID = 512
W = 256
BS = 128
HOPS = 3
ROWS_DEV = 128
NODES = 32768
GR = 16
GC = 16
BLK_DEV = 128
BLOCKS = 32768
N_SRC = 16
N_DST = 16


def draw_block_cols(key, part):
    pairs = N_SRC * N_DST * (GR // 2)
    keys = jax.random.split(jax.random.fold_in(key, 7), pairs)
    perms = jax.vmap(lambda sub: jax.random.permutation(sub, GC))(keys)
    return perms.reshape(BLOCKS).astype(jnp.int32)


def block_scale(rng, dims, pieces, smallest, largest):
    def one(position, blocks):
        draws = jax.random.uniform(jax.random.fold_in(jax.random.fold_in(rng, 6), position), (blocks,), jnp.float32, smallest / len(pieces), largest / len(pieces))
        return jnp.repeat(jnp.exp(draws), dims[position] // blocks).reshape((-1,) + (1,) * (len(dims) - position - 1))

    gain = one(*pieces[0])
    for cut in pieces[1:]:
        gain = gain * one(*cut)
    return gain


def centred(key, dims, deviation, limit, cuts=(), kind=jnp.bfloat16):
    result = deviation * jax.random.normal(key, dims, jnp.float32)
    if cuts:
        result = result * block_scale(key, dims, cuts, -0.22, 0.18)
    return jnp.clip(result, -limit, limit).astype(kind)


def setup_inputs(seed: int = 0) -> dict:
    key_list = jax.random.split(jax.random.key(seed), 7)
    raw = centred(key_list[0], (NODES, F_IN), 1.0, 6.0, ((0, 256),))
    enc_w1 = centred(key_list[1], (F_IN, HID), F_IN ** -0.5, 0.375)
    enc_w2 = centred(key_list[2], (HID, W), HID ** -0.5, 0.25)
    block_weights = centred(key_list[3], (BLOCKS, BS, BS), (N_SRC * N_DST * ROWS_DEV // 2) ** -0.5, 0.046875, ((0, 256),), jnp.float32)
    block_cols = draw_block_cols(jax.random.fold_in(key_list[6], 71), 0)
    noise = centred(key_list[5], (HOPS, NODES, W), 0.5, 3.0, ((1, 256),))
    return {"raw": raw, "enc_w1": enc_w1, "enc_w2": enc_w2, "block_weights": block_weights, "block_cols": block_cols, "noise": noise}


def normalize_rows(z):
    return (z * lax.rsqrt(lax.optimization_barrier(jnp.mean(z * z, axis=-1, keepdims=True)) + 1e-06)).astype(jnp.bfloat16)

def reference(raw, enc_w1, enc_w2, block_weights, block_cols, noise):
    hidden = jax.nn.silu(jnp.dot(raw, enc_w1, preferred_element_type=jnp.float32)).astype(jnp.bfloat16)
    encoded = normalize_rows(jnp.dot(hidden, enc_w2, preferred_element_type=jnp.float32))
    weights = block_weights.reshape(N_SRC, N_DST, BLK_DEV, BS, BS)
    columns = block_cols.reshape(N_SRC, N_DST, BLK_DEV)
    half = GC // 2
    feats = encoded
    kept = []
    for step in range(HOPS):
        col_blocks = feats.astype(jnp.float32).reshape(N_SRC, GC, BS, W)

        def one_dest(dest):
            w_dest = lax.dynamic_index_in_dim(weights, dest, 1, keepdims=False)
            c_dest = lax.dynamic_index_in_dim(columns, dest, 1, keepdims=False)
            fetched = jax.vmap(lambda blocks, cols: jnp.take(blocks, cols, axis=0))(col_blocks, c_dest)
            prods = jnp.einsum('sbij,sbjw->sbiw', w_dest, fetched, precision=lax.Precision.HIGHEST)
            return prods.reshape(N_SRC, GR, half, BS, W).sum(axis=(0, 2)).reshape(N_SRC, ROWS_DEV, W)
        agg = lax.map(one_dest, jnp.arange(N_DST, dtype=jnp.int32))
        agg = jnp.transpose(agg, (1, 0, 2, 3)).reshape(NODES, W)
        feats = normalize_rows(agg + noise[step].astype(jnp.float32))
        kept.append(feats)
    return (encoded, jnp.stack(kept))
```

```python
import jax
import jax.numpy as jnp
import numpy as np
from jax import lax
from jax.experimental import pallas as pl
from jax.experimental.pallas import tpu as pltpu
from jax.sharding import PartitionSpec as P

HOPS = 3
BS = 128
BF = jnp.bfloat16
F32 = jnp.float32

NY, NX, NZ = 4, 2, 8
YX_GROUPS = [[2 * i + c for i in range(NY * NX)] for c in range(2)]
ARRIVAL = (
    [(o, 0) for o in (0, -3, 3)]
    + [(o, 1) for o in (0, -3, 3)]
    + [(o, 0) for o in (-1, -4, 2)]
    + [(o, 1) for o in (-1, -4, 2)]
    + [(o, 0) for o in (1, -2)]
    + [(o, 1) for o in (1, -2)]
)


def shift_dst(x, dz, flip=0):
    perm = [(i, ((i // 2 + dz) % NZ) * 2 + ((i % 2) ^ flip)) for i in range(NZ * 2)]
    return lax.ppermute(x, "dst", perm)


def swap_core(x):
    return lax.ppermute(x, "src", [(i, i ^ 1) for i in range(NY * NX * 2)])


def normalize_rows(z):
    return (z * lax.rsqrt(jnp.mean(z * z, axis=-1, keepdims=True) + 1e-06)).astype(BF)


def pack_kernel(row_ref, col_ref, w_ref, o_ref):
    r = pl.program_id(0)
    o_ref[...] = jnp.zeros_like(o_ref)
    for j in range(8):
        at = pl.multiple_of(col_ref[r * 8 + j] * BS, BS)
        o_ref[:, pl.ds(at, BS)] = w_ref[j].astype(BF)


def pack(weights, row_slot, col_slot):
    rows = weights.shape[0] // 8
    return pl.pallas_call(
        pack_kernel,
        out_shape=jax.ShapeDtypeStruct((rows * BS, 16 * BS), BF),
        grid_spec=pltpu.PrefetchScalarGridSpec(
            num_scalar_prefetch=2,
            grid=(rows,),
            in_specs=[pl.BlockSpec((8, BS, BS), lambda r, rs, cs: (r, 0, 0))],
            out_specs=pl.BlockSpec((BS, 16 * BS), lambda r, rs, cs: (rs[r], 0)),
        ),
        cost_estimate=pl.CostEstimate(flops=0, bytes_accessed=16 * 2**20, transcendentals=0),
        name="pack",
    )(row_slot, col_slot, weights)


def gather_dst(h):
    g = jnp.concatenate([h, shift_dst(h, 3), shift_dst(h, -3)])
    near = jnp.concatenate([g, shift_dst(g, 0, 1)])
    up = shift_dst(near, 1)
    down = shift_dst(jnp.concatenate([near[:256], near[384:640]]), -1)
    return near, up, down


def shards(raw, enc_w1, enc_w2, block_weights, block_cols, noise):
    hidden = jax.nn.silu(jnp.dot(raw, enc_w1, preferred_element_type=F32)).astype(BF)
    encoded = normalize_rows(jnp.dot(hidden, enc_w2, preferred_element_type=F32))

    s, d = lax.axis_index("src"), lax.axis_index("dst")
    z, xh, core = d // 2, d % 2, s % 2
    off = np.array([o for o, _ in ARRIVAL], np.int32)
    flip = np.array([f for _, f in ARRIVAL], np.int32)
    held = ((z + off + NZ) % NZ) * 2 + (xh ^ flip)
    slot_of = jnp.sum(
        jnp.where(held[None, :] == jnp.arange(16)[:, None], jnp.arange(16)[None, :], 0), axis=1
    )
    col_slot = jnp.sum(
        jnp.where(block_cols[:, None] == jnp.arange(16)[None, :], slot_of[None, :], 0), axis=1
    ).astype(jnp.int32)
    r = np.arange(16, dtype=np.int32)
    row_slot = (jnp.where((r % 2) == core, 8, 0) + r // 2).astype(jnp.int32)
    a = pack(block_weights, row_slot, col_slot)

    half = a.shape[0] // 2
    feats = encoded
    kept = []
    for step in range(HOPS):
        near, up, down = gather_dst(feats)
        n1, n2 = near.shape[0], near.shape[0] + up.shape[0]
        rest = jnp.concatenate([up, down])

        def rows(lo, hi):
            return jnp.dot(a[lo:hi, :n1], near, preferred_element_type=F32) + jnp.dot(
                a[lo:hi, n1:], rest, preferred_element_type=F32
            )

        other = swap_core(rows(0, half).astype(BF))
        mine = rows(half, 2 * half) + other.astype(F32)
        parts = lax.all_to_all(
            mine.astype(BF).reshape(NY * NX, BS, -1), "src", 0, 0, axis_index_groups=YX_GROUPS
        )
        total = parts.astype(F32).sum(axis=0) + noise[step].astype(F32)
        feats = normalize_rows(total)
        kept.append(feats)
    return (encoded, jnp.stack(kept))


def solution(mesh):
    placed = (
        P(("src", "dst"), None),
        P(),
        P(),
        P(("src", "dst"), None, None),
        P(("src", "dst")),
        P(None, ("src", "dst"), None),
    )
    return jax.shard_map(
        shards,
        mesh=mesh,
        in_specs=placed,
        out_specs=(P(("src", "dst"), None), P(None, ("src", "dst"), None)),
        check_vma=False,
    )
```

```python
import functools

import jax
import jax.numpy as jnp
from jax import lax
from jax.experimental import pallas as pl
from jax.experimental.pallas import tpu as pltpu
from jax.sharding import PartitionSpec as P

HOPS = 3
BS = 128
BF = jnp.bfloat16
F32 = jnp.float32

NY, NX, NZ = 4, 2, 8
YX_GROUPS = [[2 * i + c for i in range(NY * NX)] for c in range(2)]
ARRIVAL = [
    (o, f)
    for f, offsets in (
        (0, (0, -3, 3)),
        (1, (0, -3, 3)),
        (0, (-1, -4, 2)),
        (0, (1, -2)),
        (1, (-1, -4, 2)),
        (1, (1, -2)),
    )
    for o in offsets
]


def shift_dst(x, dz, flip=0):
    perm = [(i, ((i // 2 + dz) % NZ) * 2 + ((i % 2) ^ flip)) for i in range(NZ * 2)]
    return lax.ppermute(x, "dst", perm)


def swap_core(x):
    return lax.ppermute(x, "src", [(i, i ^ 1) for i in range(NY * NX * 2)])


def normalize_rows(z):
    return (z * lax.rsqrt(jnp.mean(z * z, axis=-1, keepdims=True) + 1e-06)).astype(BF)


SLOTS = {
    f: sum(k << (4 * (o % NZ)) for k, (o, g) in enumerate(ARRIVAL) if g == f) for f in (0, 1)
}


def as_int32(v):
    return v - 2**32 if v >= 2**31 else v


def pack_kernel(other, info_ref, w_ref, *refs):
    n = (len(refs) - 1) // 2
    passed, o_ref, passed_out = refs[:n], refs[n], refs[n + 1 :]
    p = pl.program_id(0)
    core, z, xh = info_ref[0], info_ref[1], info_ref[2]

    @pl.when(p == 0)
    def _():
        for i, o in zip(passed, passed_out):
            o[...] = i[...]

    row = pl.multiple_of(p * BS, BS)
    first = 3 + (2 * p + ((core ^ other) & 1)) * 8
    o_ref[pl.ds(row, BS), :] = jnp.zeros((BS, o_ref.shape[1]), BF)
    for j in range(8):
        col = info_ref[first + j]
        table = jnp.where(
            (col & 1) == xh, jnp.int32(as_int32(SLOTS[0])), jnp.int32(as_int32(SLOTS[1]))
        )
        shift = (((col >> 1) - z) & (NZ - 1)) * 4
        at = pl.multiple_of(((table >> shift) & 15) * BS, BS)
        o_ref[pl.ds(row, BS), pl.ds(at, BS)] = w_ref[0, 0, j].astype(BF)


def pack(weights, info, other, *passed):
    pairs = weights.shape[0] // 16
    blocks = weights.reshape(pairs, 2, 8, BS, BS)
    whole = pl.BlockSpec(memory_space=pltpu.VMEM)
    return pl.pallas_call(
        functools.partial(pack_kernel, other),
        out_shape=[jax.ShapeDtypeStruct((pairs * BS, 16 * BS), BF)]
        + [jax.ShapeDtypeStruct(x.shape, x.dtype) for x in passed],
        grid_spec=pltpu.PrefetchScalarGridSpec(
            num_scalar_prefetch=1,
            grid=(pairs,),
            in_specs=[
                pl.BlockSpec((1, 1, 8, BS, BS), lambda p, i: (p, (i[0] ^ other) & 1, 0, 0, 0))
            ]
            + [whole] * len(passed),
            out_specs=[whole] * (1 + len(passed)),
        ),
        cost_estimate=pl.CostEstimate(flops=0, bytes_accessed=6 * 2**20, transcendentals=0),
        compiler_params=pltpu.CompilerParams(vmem_limit_bytes=16 * 2**20),
        name="pack",
    )(info, blocks, *passed)


def far_phase(h):
    return shift_dst(h, 3), shift_dst(h, -3)


def gather_dst(h, low, high):
    g = jnp.concatenate([h, low, high])
    x = shift_dst(g, 0, 1)
    up, down = shift_dst(g, 1), shift_dst(g[: 2 * BS], -1)
    early = jnp.concatenate([g, x, up, down])
    late = jnp.concatenate([shift_dst(x, 1), shift_dst(x[: 2 * BS], -1)])
    return early, late


def shards(raw, enc_w1, enc_w2, block_weights, block_cols, noise):
    hidden = jax.nn.silu(jnp.dot(raw, enc_w1, preferred_element_type=F32)).astype(BF)
    encoded = normalize_rows(jnp.dot(hidden, enc_w2, preferred_element_type=F32))

    s, d = lax.axis_index("src"), lax.axis_index("dst")
    info = jnp.concatenate([jnp.stack([s % 2, d // 2, d % 2]).astype(jnp.int32), block_cols])
    low, high = far_phase(encoded)
    other_rows, own = pack(block_weights, info, 1, encoded)
    (own_rows,) = pack(block_weights, info, 0)

    kept = []
    for step in range(HOPS):
        near, rest = gather_dst(own, low, high)
        n = near.shape[0]

        def early(a):
            return lax.optimization_barrier(
                jnp.dot(a[:, :n], near, preferred_element_type=F32)
            )

        def late(a):
            return jnp.dot(a[:, n:], rest, preferred_element_type=F32)

        early_other, early_own = early(other_rows), early(own_rows)
        other = swap_core((early_other + late(other_rows)).astype(BF))
        mine = early_own + late(own_rows) + other.astype(F32)
        parts = lax.all_to_all(
            mine.astype(BF).reshape(NY * NX, BS, -1), "src", 0, 0, axis_index_groups=YX_GROUPS
        )
        total = parts.astype(F32).sum(axis=0) + noise[step].astype(F32)
        own = normalize_rows(total)
        kept.append(own)
        if step < HOPS - 1:
            low, high = far_phase(own)
    return (encoded, jnp.stack(kept))


def solution(mesh):
    placed = (
        P(("src", "dst"), None),
        P(),
        P(),
        P(("src", "dst"), None, None),
        P(("src", "dst")),
        P(None, ("src", "dst"), None),
    )
    return jax.shard_map(
        shards,
        mesh=mesh,
        in_specs=placed,
        out_specs=(P(("src", "dst"), None), P(None, ("src", "dst"), None)),
        check_vma=False,
    )
```

```python
import functools

import jax
import jax.numpy as jnp
from jax import lax
from jax.experimental import pallas as pl
from jax.experimental.pallas import tpu as pltpu
from jax.sharding import PartitionSpec as P

HOPS = 3
BS = 128
BF = jnp.bfloat16
F32 = jnp.float32

NY, NX, NZ = 4, 2, 8
YX_GROUPS = [[2 * i + c for i in range(NY * NX)] for c in range(2)]
ARRIVAL = [
    (o, f)
    for f, offsets in (
        (0, (0, 3, -2)),
        (1, (0, 3, -2)),
        (0, (-1, 2, -3)),
        (0, (1, 4)),
        (1, (-1, 2, -3)),
        (1, (1, 4)),
    )
    for o in offsets
]


def shift_dst(x, dz, flip=0):
    perm = [(i, ((i // 2 + dz) % NZ) * 2 + ((i % 2) ^ flip)) for i in range(NZ * 2)]
    return lax.ppermute(x, "dst", perm)


def swap_core(x):
    return lax.ppermute(x, "src", [(i, i ^ 1) for i in range(NY * NX * 2)])


def normalize_rows(z):
    return (z * lax.rsqrt(jnp.mean(z * z, axis=-1, keepdims=True) + 1e-06)).astype(BF)


SLOTS = {
    f: sum(k << (4 * (o % NZ)) for k, (o, g) in enumerate(ARRIVAL) if g == f) for f in (0, 1)
}


def as_int32(v):
    return v - 2**32 if v >= 2**31 else v


def pack_kernel(other, info_ref, w_ref, *refs):
    n = (len(refs) - 1) // 2
    passed, o_ref, passed_out = refs[:n], refs[n], refs[n + 1 :]
    p = pl.program_id(0)
    core, z, xh = info_ref[0], info_ref[1], info_ref[2]

    @pl.when(p == 0)
    def _():
        for i, o in zip(passed, passed_out):
            o[...] = i[...]

    row = pl.multiple_of(p * BS, BS)
    first = 3 + (2 * p + ((core ^ other) & 1)) * 8
    o_ref[pl.ds(row, BS), :] = jnp.zeros((BS, o_ref.shape[1]), BF)
    for j in range(8):
        col = info_ref[first + j]
        table = jnp.where(
            (col & 1) == xh, jnp.int32(as_int32(SLOTS[0])), jnp.int32(as_int32(SLOTS[1]))
        )
        shift = (((col >> 1) - z) & (NZ - 1)) * 4
        at = pl.multiple_of(((table >> shift) & 15) * BS, BS)
        o_ref[pl.ds(row, BS), pl.ds(at, BS)] = w_ref[0, 0, j].astype(BF)


def pack(weights, info, other, *passed):
    pairs = weights.shape[0] // 16
    blocks = weights.reshape(pairs, 2, 8, BS, BS)
    whole = pl.BlockSpec(memory_space=pltpu.VMEM)
    return pl.pallas_call(
        functools.partial(pack_kernel, other),
        out_shape=[jax.ShapeDtypeStruct((pairs * BS, 16 * BS), BF)]
        + [jax.ShapeDtypeStruct(x.shape, x.dtype) for x in passed],
        grid_spec=pltpu.PrefetchScalarGridSpec(
            num_scalar_prefetch=1,
            grid=(pairs,),
            in_specs=[
                pl.BlockSpec((1, 1, 8, BS, BS), lambda p, i: (p, (i[0] ^ other) & 1, 0, 0, 0))
            ]
            + [whole] * len(passed),
            out_specs=[whole] * (1 + len(passed)),
        ),
        cost_estimate=pl.CostEstimate(flops=0, bytes_accessed=6 * 2**20, transcendentals=0),
        compiler_params=pltpu.CompilerParams(vmem_limit_bytes=16 * 2**20),
        name="pack",
    )(info, blocks, *passed)


def far_phase(h):
    return shift_dst(h, -3), shift_dst(h, 2)


def gather_dst(h, low, high):
    g = jnp.concatenate([h, low, high])
    x = shift_dst(g, 0, 1)
    up, down = shift_dst(g, 1), shift_dst(g[: 2 * BS], -1)
    early = jnp.concatenate([g, x, up, down])
    late = jnp.concatenate([shift_dst(x, 1), shift_dst(x[: 2 * BS], -1)])
    return early, late


def shards(raw, enc_w1, enc_w2, block_weights, block_cols, noise):
    hidden = jax.nn.silu(jnp.dot(raw, enc_w1, preferred_element_type=F32)).astype(BF)
    encoded = normalize_rows(jnp.dot(hidden, enc_w2, preferred_element_type=F32))

    s, d = lax.axis_index("src"), lax.axis_index("dst")
    info = jnp.concatenate([jnp.stack([s % 2, d // 2, d % 2]).astype(jnp.int32), block_cols])
    low, high = far_phase(encoded)
    other_rows, own = pack(block_weights, info, 1, encoded)
    (own_rows,) = pack(block_weights, info, 0)

    kept = []
    for step in range(HOPS):
        near, rest = gather_dst(own, low, high)
        n = near.shape[0]

        def early(a):
            return lax.optimization_barrier(
                jnp.dot(a[:, :n], near, preferred_element_type=F32)
            )

        def late(a):
            return jnp.dot(a[:, n:], rest, preferred_element_type=F32)

        early_other, early_own = early(other_rows), early(own_rows)
        other = swap_core((early_other + late(other_rows)).astype(BF))
        mine = early_own + late(own_rows) + other.astype(F32)
        parts = lax.all_to_all(
            mine.astype(BF).reshape(NY * NX, BS, -1), "src", 0, 0, axis_index_groups=YX_GROUPS
        )
        total = parts.astype(F32).sum(axis=0) + noise[step].astype(F32)
        own = normalize_rows(total)
        kept.append(own)
        if step < HOPS - 1:
            low, high = far_phase(own)
    return (encoded, jnp.stack(kept))


def solution(mesh):
    placed = (
        P(("src", "dst"), None),
        P(),
        P(),
        P(("src", "dst"), None, None),
        P(("src", "dst")),
        P(None, ("src", "dst"), None),
    )
    return jax.shard_map(
        shards,
        mesh=mesh,
        in_specs=placed,
        out_specs=(P(("src", "dst"), None), P(None, ("src", "dst"), None)),
        check_vma=False,
    )
```

```python
import functools

import jax
import jax.numpy as jnp
from jax import lax
from jax.experimental import pallas as pl
from jax.experimental.pallas import tpu as pltpu
from jax.sharding import PartitionSpec as P

HOPS = 3
BS = 128
BF = jnp.bfloat16
F32 = jnp.float32

NY, NX, NZ = 4, 2, 8
YX_GROUPS = [[2 * i + c for i in range(NY * NX)] for c in range(2)]
ARRIVAL = [
    (o, f)
    for f, offsets in (
        (0, (0, 3, -2)),
        (1, (0, 3, -2)),
        (0, (-1, 2, -3)),
        (0, (1, 4)),
        (1, (-1, 2, -3)),
        (1, (1, 4)),
    )
    for o in offsets
]


def shift_dst(x, dz, flip=0):
    perm = []
    for s in range(NY * NX * 2):
        step = -dz if s % 2 else dz
        for d in range(NZ * 2):
            to = ((d // 2 + step) % NZ) * 2 + ((d % 2) ^ flip)
            perm.append((s * NZ * 2 + d, s * NZ * 2 + to))
    return lax.ppermute(x, ("src", "dst"), perm)


def swap_core(x):
    return lax.ppermute(x, "src", [(i, i ^ 1) for i in range(NY * NX * 2)])


def normalize_rows(z):
    return (z * lax.rsqrt(jnp.mean(z * z, axis=-1, keepdims=True) + 1e-06)).astype(BF)


SLOTS = {
    f: sum(k << (4 * (o % NZ)) for k, (o, g) in enumerate(ARRIVAL) if g == f) for f in (0, 1)
}


def as_int32(v):
    return v - 2**32 if v >= 2**31 else v


def pack_kernel(other, info_ref, w_ref, *refs):
    n = (len(refs) - 1) // 2
    passed, o_ref, passed_out = refs[:n], refs[n], refs[n + 1 :]
    p = pl.program_id(0)
    core, z, xh = info_ref[0], info_ref[1], info_ref[2]

    @pl.when(p == 0)
    def _():
        for i, o in zip(passed, passed_out):
            o[...] = i[...]

    row = pl.multiple_of(p * BS, BS)
    first = 3 + (2 * p + ((core ^ other) & 1)) * 8
    o_ref[pl.ds(row, BS), :] = jnp.zeros((BS, o_ref.shape[1]), BF)
    for j in range(8):
        col = info_ref[first + j]
        table = jnp.where(
            (col & 1) == xh, jnp.int32(as_int32(SLOTS[0])), jnp.int32(as_int32(SLOTS[1]))
        )
        shift = (((col >> 1) - z) * (1 - 2 * core) & (NZ - 1)) * 4
        at = pl.multiple_of(((table >> shift) & 15) * BS, BS)
        o_ref[pl.ds(row, BS), pl.ds(at, BS)] = w_ref[0, 0, j].astype(BF)


def pack(weights, info, other, *passed):
    pairs = weights.shape[0] // 16
    blocks = weights.reshape(pairs, 2, 8, BS, BS)
    whole = pl.BlockSpec(memory_space=pltpu.VMEM)
    return pl.pallas_call(
        functools.partial(pack_kernel, other),
        out_shape=[jax.ShapeDtypeStruct((pairs * BS, 16 * BS), BF)]
        + [jax.ShapeDtypeStruct(x.shape, x.dtype) for x in passed],
        grid_spec=pltpu.PrefetchScalarGridSpec(
            num_scalar_prefetch=1,
            grid=(pairs,),
            in_specs=[
                pl.BlockSpec((1, 1, 8, BS, BS), lambda p, i: (p, (i[0] ^ other) & 1, 0, 0, 0))
            ]
            + [whole] * len(passed),
            out_specs=[whole] * (1 + len(passed)),
        ),
        cost_estimate=pl.CostEstimate(flops=0, bytes_accessed=6 * 2**20, transcendentals=0),
        compiler_params=pltpu.CompilerParams(vmem_limit_bytes=16 * 2**20),
        name="pack",
    )(info, blocks, *passed)


def far_phase(h):
    return shift_dst(h, -3), shift_dst(h, 2)


def gather_dst(h, low, high):
    g = jnp.concatenate([h, low, high])
    x = shift_dst(g, 0, 1)
    up, down = shift_dst(g, 1), shift_dst(g[: 2 * BS], -1)
    early = jnp.concatenate([g, x, up, down])
    late = jnp.concatenate([shift_dst(x, 1), shift_dst(x[: 2 * BS], -1)])
    return early, late


def shards(raw, enc_w1, enc_w2, block_weights, block_cols, noise):
    hidden = jax.nn.silu(jnp.dot(raw, enc_w1, preferred_element_type=F32)).astype(BF)
    encoded = normalize_rows(jnp.dot(hidden, enc_w2, preferred_element_type=F32))

    s, d = lax.axis_index("src"), lax.axis_index("dst")
    info = jnp.concatenate([jnp.stack([s % 2, d // 2, d % 2]).astype(jnp.int32), block_cols])
    low, high = far_phase(encoded)
    other_rows, own = pack(block_weights, info, 1, encoded)
    (own_rows,) = pack(block_weights, info, 0)

    kept = []
    for step in range(HOPS):
        near, rest = gather_dst(own, low, high)
        n = near.shape[0]

        def early(a):
            return lax.optimization_barrier(
                jnp.dot(a[:, :n], near, preferred_element_type=F32)
            )

        def late(a):
            return jnp.dot(a[:, n:], rest, preferred_element_type=F32)

        early_other, early_own = early(other_rows), early(own_rows)
        other = swap_core((early_other + late(other_rows)).astype(BF))
        mine = early_own + late(own_rows) + other.astype(F32)
        parts = lax.all_to_all(
            mine.astype(BF).reshape(NY * NX, BS, -1), "src", 0, 0, axis_index_groups=YX_GROUPS
        )
        total = parts.astype(F32).sum(axis=0) + noise[step].astype(F32)
        own = normalize_rows(total)
        kept.append(own)
        if step < HOPS - 1:
            low, high = far_phase(own)
    return (encoded, jnp.stack(kept))


def solution(mesh):
    placed = (
        P(("src", "dst"), None),
        P(),
        P(),
        P(("src", "dst"), None, None),
        P(("src", "dst")),
        P(None, ("src", "dst"), None),
    )
    return jax.shard_map(
        shards,
        mesh=mesh,
        in_specs=placed,
        out_specs=(P(("src", "dst"), None), P(None, ("src", "dst"), None)),
        check_vma=False,
    )
```

```python
import functools

import jax
import jax.numpy as jnp
from jax import lax
from jax.experimental import pallas as pl
from jax.experimental.pallas import tpu as pltpu
from jax.sharding import PartitionSpec as P

HOPS = 3
BS = 128
BF = jnp.bfloat16
F32 = jnp.float32

NY, NX, NZ = 4, 2, 8
YX_GROUPS = [[2 * i + c for i in range(NY * NX)] for c in range(2)]
ARRIVAL = [
    (0, 0), (0, 1), (3, 0), (-2, 0), (3, 1), (-2, 1),
    (-1, 0), (-1, 1), (2, 0), (-3, 0), (1, 0), (1, 1), (4, 0),
    (2, 1), (-3, 1), (4, 1),
]


def shift_dst(x, dz, flip=0):
    perm = [(i, ((i // 2 + dz) % NZ) * 2 + ((i % 2) ^ flip)) for i in range(NZ * 2)]
    return lax.ppermute(x, "dst", perm)


def swap_core(x):
    return lax.ppermute(x, "src", [(i, i ^ 1) for i in range(NY * NX * 2)])


def normalize_rows(z):
    return (z * lax.rsqrt(jnp.mean(z * z, axis=-1, keepdims=True) + 1e-06)).astype(BF)


SLOTS = {
    f: sum(k << (4 * (o % NZ)) for k, (o, g) in enumerate(ARRIVAL) if g == f) for f in (0, 1)
}


def as_int32(v):
    return v - 2**32 if v >= 2**31 else v


def pack_kernel(other, info_ref, w_ref, *refs):
    n = (len(refs) - 1) // 2
    passed, o_ref, passed_out = refs[:n], refs[n], refs[n + 1 :]
    p = pl.program_id(0)
    core, z, xh = info_ref[0], info_ref[1], info_ref[2]

    @pl.when(p == 0)
    def _():
        for i, o in zip(passed, passed_out):
            o[...] = i[...]

    row = pl.multiple_of(p * BS, BS)
    first = 3 + (2 * p + ((core ^ other) & 1)) * 8
    o_ref[pl.ds(row, BS), :] = jnp.zeros((BS, o_ref.shape[1]), BF)
    for j in range(8):
        col = info_ref[first + j]
        table = jnp.where(
            (col & 1) == xh, jnp.int32(as_int32(SLOTS[0])), jnp.int32(as_int32(SLOTS[1]))
        )
        shift = (((col >> 1) - z) & (NZ - 1)) * 4
        at = pl.multiple_of(((table >> shift) & 15) * BS, BS)
        o_ref[pl.ds(row, BS), pl.ds(at, BS)] = w_ref[0, 0, j].astype(BF)


def pack(weights, info, other, *passed):
    pairs = weights.shape[0] // 16
    blocks = weights.reshape(pairs, 2, 8, BS, BS)
    whole = pl.BlockSpec(memory_space=pltpu.VMEM)
    return pl.pallas_call(
        functools.partial(pack_kernel, other),
        out_shape=[jax.ShapeDtypeStruct((pairs * BS, 16 * BS), BF)]
        + [jax.ShapeDtypeStruct(x.shape, x.dtype) for x in passed],
        grid_spec=pltpu.PrefetchScalarGridSpec(
            num_scalar_prefetch=1,
            grid=(pairs,),
            in_specs=[
                pl.BlockSpec((1, 1, 8, BS, BS), lambda p, i: (p, (i[0] ^ other) & 1, 0, 0, 0))
            ]
            + [whole] * len(passed),
            out_specs=[whole] * (1 + len(passed)),
        ),
        cost_estimate=pl.CostEstimate(flops=0, bytes_accessed=6 * 2**20, transcendentals=0),
        compiler_params=pltpu.CompilerParams(vmem_limit_bytes=16 * 2**20),
        name="pack",
    )(info, blocks, *passed)


def far_phase(h):
    return shift_dst(h, 0, 1), shift_dst(h, -3), shift_dst(h, 2)


def gather_dst(h, pair, low, high):
    x = shift_dst(jnp.concatenate([low, high]), 0, 1)
    q = jnp.concatenate([h, pair, low, high])
    up, down = shift_dst(q, 1), shift_dst(q[: 3 * BS], -1)
    early = jnp.concatenate([q, x, up, down])
    late = jnp.concatenate([shift_dst(x, 1), shift_dst(x[:BS], -1)])
    return early, late


def shards(raw, enc_w1, enc_w2, block_weights, block_cols, noise):
    hidden = jax.nn.silu(jnp.dot(raw, enc_w1, preferred_element_type=F32)).astype(BF)
    encoded = normalize_rows(jnp.dot(hidden, enc_w2, preferred_element_type=F32))

    s, d = lax.axis_index("src"), lax.axis_index("dst")
    info = jnp.concatenate([jnp.stack([s % 2, d // 2, d % 2]).astype(jnp.int32), block_cols])
    far = far_phase(encoded)
    other_rows, own = pack(block_weights, info, 1, encoded)
    (own_rows,) = pack(block_weights, info, 0)

    kept = []
    for step in range(HOPS):
        near, rest = gather_dst(own, *far)
        n = near.shape[0]

        def early(a):
            return lax.optimization_barrier(
                jnp.dot(a[:, :n], near, preferred_element_type=F32)
            )

        def late(a):
            return jnp.dot(a[:, n:], rest, preferred_element_type=F32)

        early_other, early_own = early(other_rows), early(own_rows)
        other = swap_core((early_other + late(other_rows)).astype(BF))
        mine = early_own + late(own_rows) + other.astype(F32)
        parts = lax.all_to_all(
            mine.astype(BF).reshape(NY * NX, BS, -1), "src", 0, 0, axis_index_groups=YX_GROUPS
        )
        total = parts.astype(F32).sum(axis=0) + noise[step].astype(F32)
        own = normalize_rows(total)
        kept.append(own)
        if step < HOPS - 1:
            far = far_phase(own)
    return (encoded, jnp.stack(kept))


def solution(mesh):
    placed = (
        P(("src", "dst"), None),
        P(),
        P(),
        P(("src", "dst"), None, None),
        P(("src", "dst")),
        P(None, ("src", "dst"), None),
    )
    return jax.shard_map(
        shards,
        mesh=mesh,
        in_specs=placed,
        out_specs=(P(("src", "dst"), None), P(None, ("src", "dst"), None)),
        check_vma=False,
    )
```
